512 devices in a mesh: expert: 128 (over z, y, core), token: 4 (over x).
Axes of the slice: x: 4, y: 4, z: 16, core: 2. Of those that a mesh axis runs over, the one named last changes fastest.
Arguments:
- tokens: bfloat16 [8192, 2048], P(('expert', 'token')), may hold values from -6 to 6
- routes: int32 [8192, 8], P(('expert', 'token')), may hold values from 0 to 127, all different within a row; in each aligned block of 16 rows (0 to 15, 16 to 31, ...) at most 2 rows name the same one
- assign: int32 [128], replicated, may hold values from 0 to 31, as said below
- gate_weight: bfloat16 [128, 2048, 1536], P('expert', None, 'token'), may hold values from -0.125 to 0.125
- up_weight: bfloat16 [128, 2048, 1536], P('expert', None, 'token'), may hold values from -0.125 to 0.125
- sketch: bfloat16 [128, 1536, 512], P('expert', 'token'), may hold values from -6 to 6
Outputs:
- hidden: bfloat16 [128, 1024, 1536], P('expert', None, 'token')
The draws below stay inside these ranges and needn't reach their ends.
Inputs may be any that keep to these rules, and one draw needn't show every extreme that they name: `routes`: within each aligned block of 16 tokens each token names 8 different experts, and no expert is named by more than 2 entries of the block. `assign`: every one of the 32 clusters has at least two experts.
All inputs are finite; a program needn't handle non-finite values.
Results may differ from the reference program's by a relative error of at most 0.029.
Values may be sent and summed in bfloat16 or wider, within the bound.
A program may use at most 64 MiB of HBM per device.

```python
import math
import jax
import jax.numpy as jnp
import numpy as np
from jax import lax

D = 2048
FF = 1536
R = 512
TOP = 8
ITERS = 1
TOK_DEV = 16
EXPERTS = 128
CLUSTERS = 32
CAP = 2
SLOTS = 1024
TOKENS = 8192
N_TOKEN = 4


def draw_assign(key, part):
    cluster_count = CLUSTERS
    extra_total = EXPERTS - 2 * cluster_count
    head_extra = min(6, extra_total)
    rest_extra = extra_total - head_extra
    base_key = jax.random.fold_in(key, 11)
    key_slots = jax.random.fold_in(base_key, 1)
    key_labels = jax.random.fold_in(base_key, 2)
    key_experts = jax.random.fold_in(base_key, 3)
    slot_order = jax.random.permutation(key_slots, 6 * (cluster_count - 1))
    chosen = (slot_order < rest_extra).astype(jnp.int32).reshape(cluster_count - 1, 6).sum(axis=1)
    cluster_sizes = jnp.concatenate([jnp.full((1,), 2 + head_extra, jnp.int32), 2 + chosen])
    bounds = jnp.cumsum(cluster_sizes)
    position = jnp.arange(EXPERTS, dtype=jnp.int32)
    cluster_of = jnp.sum((position[:, None] >= bounds[None, :]).astype(jnp.int32), axis=1)
    labels = jax.random.permutation(key_labels, cluster_count).astype(jnp.int32)
    expert_order = jax.random.permutation(key_experts, EXPERTS)
    return jnp.zeros((EXPERTS,), jnp.int32).at[expert_order].set(labels[cluster_of])


def level_of(own_key, extent, shards, smallest, top_value):
    gain, own = 1.0, jax.random.fold_in(own_key, 6)
    for dim, shards_of in shards:
        draws = jnp.exp(jax.random.uniform(jax.random.fold_in(own, dim), (shards_of,), jnp.float32, smallest / len(shards), top_value / len(shards)))
        gain = gain * jnp.repeat(draws, extent[dim] // shards_of).reshape([-1 if axis == dim else 1 for axis in range(len(extent))])
    return gain


def assign_block(stream_key, own, number, rows, number_of, top, bound, skew):
    order = jax.random.permutation(stream_key, number_of)
    heavy_load, usual = load_shares(number_of, rows * top, bound, skew, True), load_shares(number_of, rows * top, bound, skew, False)
    places = jnp.arange(number_of)

    def named(tallies, offset_by):
        used = int((tallies > 0).sum())
        fixed = max(1, used // 4)
        moved = fixed + (places - fixed + offset_by * (used - fixed)) % max(1, number_of - fixed)
        return jnp.zeros((number_of,), jnp.int32).at[order[jnp.where(places < fixed, places, moved)]].set(jnp.asarray(tallies, jnp.int32))

    tallies = jnp.where(number % 4 == 0, named(heavy_load, number // 4), named(usual, number - number // 4 - 1))
    mixed = jax.random.permutation(jax.random.fold_in(own, 3), number_of)
    giver, sink = mixed[0:number_of // 2 * 2:2], mixed[1:number_of // 2 * 2:2]
    margin = jnp.minimum(tallies[giver] - 1, bound - tallies[sink]) // 2
    margin = jnp.where((giver == order[0]) | (sink == order[0]) | (tallies[sink] == 0), 0, jnp.maximum(margin, 0))
    moved = jax.random.randint(jax.random.fold_in(own, 4), (number_of // 2,), 0, 1 << 20) % (margin + 1)
    tallies = tallies.at[giver].add(-moved).at[sink].add(moved)
    members = jnp.searchsorted(jnp.cumsum(tallies), jnp.arange(rows * top), side="right").astype(jnp.int32)
    listing = members.reshape(top, rows).T
    listing = listing[jax.random.permutation(jax.random.fold_in(own, 1), rows)]
    offset_by = jax.random.randint(jax.random.fold_in(own, 2), (rows, 1), 0, top)
    return jnp.take_along_axis(listing, (jnp.arange(top)[None, :] + offset_by) % top, axis=1)


def load_shares(count, total, reach, lean, full):
    portions = [(1 << 20) // math.isqrt(rank ** lean) + 1 for rank in range(1, count + 1)]
    largest = reach if full else min(reach, max(-(-total // count), total * portions[0] // sum(portions)))
    least = 1 if total - largest >= count - 1 else 0
    given, surplus = [largest] + [least] * (count - 1), total - largest - least * (count - 1)
    while surplus > 0:
        free = [i for i in range(1, count) if given[i] < largest] or [i for i in range(1, count) if given[i] < reach]
        mass, left = sum([portions[i] for i in free]), surplus
        for i in free:
            addition = min(reach - given[i], max(1, left * portions[i] // mass), surplus)
            given[i] = given[i] + addition
            surplus = surplus - addition
    return np.array(given)


def noise(key, extent, spread, most, split=(), kind=jnp.bfloat16):
    drawn = spread * jax.random.normal(key, extent, jnp.float32)
    if split:
        drawn = drawn * level_of(key, extent, split, -0.22, 0.18)
    return jnp.clip(drawn, -most, most).astype(kind)


def setup_inputs(seed: int = 0) -> dict:
    arg_keys = jax.random.split(jax.random.key(seed), 7)
    tokens = noise(arg_keys[0], (TOKENS, D), 1.0, 6.0, ((0, 512),))
    routes_keys = jax.random.split(jax.random.fold_in(arg_keys[1], 1), TOKENS // TOK_DEV)
    routes_turns = jax.random.permutation(jax.random.fold_in(arg_keys[1], 3), TOKENS // TOK_DEV)
    routes = jax.vmap(lambda own, number: assign_block(jax.random.fold_in(arg_keys[1], 2), own, number, TOK_DEV, EXPERTS, TOP, CAP, 2))(routes_keys, routes_turns).reshape((TOKENS, TOP))
    assign = draw_assign(jax.random.fold_in(arg_keys[6], 71), 0)
    gate_weight = noise(arg_keys[3], (EXPERTS, D, FF), D ** -0.5, 0.125, ((0, 128), (2, 4)))
    up_weight = noise(arg_keys[4], (EXPERTS, D, FF), D ** -0.5, 0.125, ((0, 128), (2, 4)))
    sketch = noise(arg_keys[5], (EXPERTS, FF, R), 1.0, 6.0, ((0, 128), (1, 4)))
    return dict(tokens=tokens, routes=routes, assign=assign, gate_weight=gate_weight, up_weight=up_weight, sketch=sketch)


def orthonormal(cluster_sum):
    rounded = lax.optimization_barrier(cluster_sum.astype(jnp.bfloat16)).astype(jnp.float32)
    column_gram = jnp.dot(rounded.T, rounded, precision=lax.Precision.HIGHEST)
    lower_factor = jnp.linalg.cholesky(column_gram)
    solved = jax.scipy.linalg.solve_triangular(lower_factor, rounded.T, lower=True)
    return solved.T.astype(jnp.bfloat16)

def split_product(weight_one, right_side):
    quarter = FF // N_TOKEN
    running = jnp.zeros((D, R), jnp.float32)
    for block in range(N_TOKEN):
        product_part = jnp.dot(weight_one[:, block * quarter:(block + 1) * quarter].astype(jnp.float32), right_side[block * quarter:(block + 1) * quarter].astype(jnp.float32), preferred_element_type=jnp.float32)
        running = running + lax.optimization_barrier(product_part.astype(jnp.bfloat16)).astype(jnp.float32)
    return running

def reference(tokens, routes, assign, gate_weight, up_weight, sketch):

    def first_term(bundle):
        return split_product(bundle[0], bundle[1])
    terms = lax.map(first_term, (up_weight, sketch))
    basis = lax.map(orthonormal, jax.ops.segment_sum(terms, assign, num_segments=CLUSTERS))
    for iteration in range(ITERS):

        def gram_term(bundle):
            weight_one, cluster = bundle
            projected = lax.dot_general(weight_one.astype(jnp.float32), basis[cluster].astype(jnp.float32), (((0,), (0,)), ((), ())), preferred_element_type=jnp.float32).astype(jnp.bfloat16)
            return split_product(weight_one, projected)
        terms = lax.map(gram_term, (up_weight, assign))
        basis = lax.map(orthonormal, jax.ops.segment_sum(terms, assign, num_segments=CLUSTERS))
    blocks = EXPERTS * N_TOKEN
    entries = TOK_DEV * TOP
    block_ids = routes.reshape(blocks, entries)
    expert_hits = (block_ids[:, :, None] == jnp.arange(EXPERTS, dtype=jnp.int32)[None, None, :]).astype(jnp.int32)
    earlier = jnp.cumsum(expert_hits, axis=1) - expert_hits
    slot_index = jnp.sum(earlier * expert_hits, axis=2).astype(jnp.int32)
    block_index = jnp.arange(blocks, dtype=jnp.int32)[:, None]
    source_expert = block_index // N_TOKEN
    source_token = block_index % N_TOKEN
    position = ((source_token * EXPERTS + source_expert) * CAP + slot_index).astype(jnp.int32)
    token_index = (block_index * TOK_DEV + jnp.arange(entries, dtype=jnp.int32)[None, :] // TOP).astype(jnp.int32)
    slots_in = jnp.zeros((EXPERTS, SLOTS, D), jnp.bfloat16).at[block_ids, position].set(tokens[token_index])

    def expert_hidden(bundle):
        slot_rows, gate_one, up_one, cluster = bundle
        shared = basis[cluster]
        on_basis = jnp.dot(slot_rows.astype(jnp.float32), shared.astype(jnp.float32), preferred_element_type=jnp.float32).astype(jnp.bfloat16)
        coefficient = lax.dot_general(shared.astype(jnp.float32), up_one.astype(jnp.float32), (((0,), (0,)), ((), ())), preferred_element_type=jnp.float32).astype(jnp.bfloat16)
        gate_value = jnp.dot(slot_rows.astype(jnp.float32), gate_one.astype(jnp.float32), preferred_element_type=jnp.float32)
        merged = jnp.dot(on_basis.astype(jnp.float32), coefficient.astype(jnp.float32), preferred_element_type=jnp.float32)
        return (jax.nn.silu(gate_value) * merged).astype(jnp.bfloat16)
    return lax.map(expert_hidden, (slots_in, gate_weight, up_weight, assign))
```

```python
import jax
import jax.numpy as jnp
from jax import lax
from jax.experimental import pallas as pl
from jax.experimental.pallas import tpu as pltpu
from jax.sharding import PartitionSpec as P

QUINTICS = (
    (6.009771924945882, -15.455931527233346, 10.973255328070678),
    (2.240850259026762, -1.6147116422452963, 0.4129695492489308),
    (1.8859120675161938, -1.2620718053405737, 0.3762092163333401),
)
DONE = 0.05**4
MOST = 60


def place_tokens(tok_rows, tok_ids, expert_count, capacity):
    flat_ids = tok_ids.reshape(-1)
    entry = jnp.arange(flat_ids.shape[0], dtype=jnp.int32)
    earlier = (flat_ids[:, None] == flat_ids[None, :]) & (entry[None, :] < entry[:, None])
    slot_index = jnp.sum(earlier.astype(jnp.int32), axis=1)
    target = flat_ids * capacity + slot_index
    select = (
        jnp.arange(expert_count * capacity, dtype=jnp.int32)[:, None] == target[None, :]
    ).astype(jnp.float32)
    select = (
        select.reshape(expert_count * capacity, tok_rows.shape[0], tok_ids.shape[1])
        .sum(axis=2)
        .astype(jnp.bfloat16)
    )
    filled = jnp.dot(select, tok_rows, preferred_element_type=jnp.float32).astype(jnp.bfloat16)
    return filled.reshape(expert_count, capacity, tok_rows.shape[1])


def dot16(a, b):
    return jnp.dot(
        a.astype(jnp.bfloat16), b.astype(jnp.bfloat16), preferred_element_type=jnp.float32
    )


def dot32(a, b, dims=(((1,), (0,)), ((), ()))):
    return lax.dot_general(
        a, b, dims, precision=lax.Precision.HIGHEST, preferred_element_type=jnp.float32
    )


def orthonormal_kernel(rows_ref, basis_ref, gram_ref, x_ref):
    rank = rows_ref.shape[1]
    gram = lax.dot_general(
        rows_ref[...], rows_ref[...], (((0,), (0,)), ((), ())), preferred_element_type=jnp.float32
    )
    eye = (
        lax.broadcasted_iota(jnp.int32, (rank, rank), 0)
        == lax.broadcasted_iota(jnp.int32, (rank, rank), 1)
    )
    diagonal = jnp.where(eye, gram, 0.0)
    down = lax.rsqrt(jnp.sum(diagonal, axis=1, keepdims=True))
    across = lax.rsqrt(jnp.sum(diagonal, axis=0, keepdims=True))
    gram = gram * down * across
    gram_ref[...] = gram
    rough = gram.astype(jnp.bfloat16)
    square = dot16(rough, rough)
    inv = lax.rsqrt(1.02 * jnp.sqrt(jnp.sum(square * square)))
    inv2 = inv * inv
    unit = eye.astype(jnp.float32)
    a, b, c = QUINTICS[0]
    x = inv * (a * unit + (b * inv2) * gram + (c * inv2 * inv2) * square)
    for a, b, c in QUINTICS[1:]:
        x16 = x.astype(jnp.bfloat16)
        s16 = dot16(x16, dot16(rough, x16)).astype(jnp.bfloat16)
        x = a * x + dot16(x16, b * s16.astype(jnp.float32) + c * dot16(s16, s16))
    x_ref[...] = x

    def unfinished(state):
        step, size = state
        return (size > DONE) & (step < MOST)

    def refine(state):
        step, _ = state
        x = x_ref[...]
        s = dot32(x, dot32(gram_ref[...], x), (((0,), (0,)), ((), ())))
        e = unit - s
        ee = dot16(e, e)
        x_ref[...] = x + dot16(x, 0.5 * e + 0.375 * ee)
        return step + 1, jnp.sum(ee * ee)

    lax.while_loop(unfinished, refine, (jnp.int32(0), jnp.float32(1.0)))
    scaled = x_ref[...] * down
    high = scaled.astype(jnp.bfloat16)
    low = (scaled - high.astype(jnp.float32)).astype(jnp.bfloat16)
    rows = rows_ref[...]
    basis_ref[...] = (
        jnp.dot(rows, high, preferred_element_type=jnp.float32)
        + jnp.dot(rows, low, preferred_element_type=jnp.float32)
    ).astype(jnp.bfloat16)


def orthonormal(cluster_rows):
    rank = cluster_rows.shape[1]
    return pl.pallas_call(
        orthonormal_kernel,
        out_shape=jax.ShapeDtypeStruct(cluster_rows.shape, jnp.bfloat16),
        in_specs=[pl.BlockSpec(memory_space=pltpu.VMEM)],
        out_specs=pl.BlockSpec(memory_space=pltpu.VMEM),
        scratch_shapes=[
            pltpu.VMEM((rank, rank), jnp.float32),
            pltpu.VMEM((rank, rank), jnp.float32),
        ],
        compiler_params=pltpu.CompilerParams(vmem_limit_bytes=48 << 20),
        cost_estimate=pl.CostEstimate(
            flops=40_000_000_000, bytes_accessed=4 << 20, transcendentals=0
        ),
        name="orthonormal",
    )(cluster_rows)


def new_basis(partial_term, same, token_count, expert_count):
    rows, rank = partial_term.shape
    block = rows // token_count // expert_count
    own = lax.psum_scatter(partial_term, "token", scatter_dimension=0, tiled=True)
    arrived = lax.all_to_all(
        own.reshape(expert_count, block * rank), "expert", split_axis=0, concat_axis=0, tiled=True
    )
    outgoing = jnp.dot(same, arrived, preferred_element_type=jnp.float32).astype(jnp.bfloat16)
    returned = lax.all_to_all(outgoing, "expert", split_axis=0, concat_axis=0, tiled=True)
    cluster_rows = lax.all_gather(
        returned.reshape(expert_count * block, rank), "token", axis=0, tiled=True
    )
    return orthonormal(cluster_rows)


def per_device(tokens, routes, assign, gate_weight, up_weight, sketch):
    expert_count = lax.axis_size("expert")
    token_count = lax.axis_size("token")
    gate_local = gate_weight[0]
    up_local = up_weight[0]
    same = (assign[None, :] == assign[:, None]).astype(jnp.bfloat16)
    partial_term = jnp.dot(up_local, sketch[0], preferred_element_type=jnp.float32).astype(
        jnp.bfloat16
    )
    basis = new_basis(partial_term, same, token_count, expert_count)
    projected = lax.dot_general(
        up_local, basis, (((0,), (0,)), ((), ())), preferred_element_type=jnp.float32
    ).astype(jnp.bfloat16)
    partial_term = jnp.dot(up_local, projected, preferred_element_type=jnp.float32).astype(
        jnp.bfloat16
    )
    basis = new_basis(partial_term, same, token_count, expert_count)
    shard_rows = tokens.shape[0]
    capacity = max(2, 2 * shard_rows * routes.shape[1] // expert_count)
    outgoing = place_tokens(tokens, routes, expert_count, capacity)
    arrived = lax.all_to_all(outgoing, "expert", split_axis=0, concat_axis=0, tiled=True)
    slots_in = lax.all_gather(arrived, "token", axis=0, tiled=True)
    slots_in = slots_in.reshape(-1, tokens.shape[1])
    gate_value = jnp.dot(slots_in, gate_local, preferred_element_type=jnp.float32)
    on_basis = jnp.dot(slots_in, basis, preferred_element_type=jnp.float32).astype(jnp.bfloat16)
    coefficient = lax.dot_general(
        basis, up_local, (((0,), (0,)), ((), ())), preferred_element_type=jnp.float32
    ).astype(jnp.bfloat16)
    merged = jnp.dot(on_basis, coefficient, preferred_element_type=jnp.float32)
    hidden = (jax.nn.silu(gate_value) * merged).astype(jnp.bfloat16)
    return hidden[None]


def solution(mesh):
    return jax.shard_map(
        per_device,
        mesh=mesh,
        in_specs=(
            P(("expert", "token"), None),
            P(("expert", "token"), None),
            P(),
            P("expert", None, "token"),
            P("expert", None, "token"),
            P("expert", "token", None),
        ),
        out_specs=P("expert", None, "token"),
        check_vma=False,
    )
```

```python
import jax
import jax.numpy as jnp
from jax import lax
from jax.experimental import pallas as pl
from jax.experimental.pallas import tpu as pltpu
from jax.sharding import PartitionSpec as P

MESH = pl.DeviceIdType.MESH

QUINTICS = (
    (6.009771924945882, -15.455931527233346, 10.973255328070678),
    (2.240850259026762, -1.6147116422452963, 0.4129695492489308),
    (1.8859120675161938, -1.2620718053405737, 0.3762092163333401),
)
DONE = 0.05**4
MOST = 60


def place_tokens(tok_rows, tok_ids, expert_count, capacity):
    flat_ids = tok_ids.reshape(-1)
    entry = jnp.arange(flat_ids.shape[0], dtype=jnp.int32)
    earlier = (flat_ids[:, None] == flat_ids[None, :]) & (entry[None, :] < entry[:, None])
    slot_index = jnp.sum(earlier.astype(jnp.int32), axis=1)
    target = flat_ids * capacity + slot_index
    select = (
        jnp.arange(expert_count * capacity, dtype=jnp.int32)[:, None] == target[None, :]
    ).astype(jnp.float32)
    select = (
        select.reshape(expert_count * capacity, tok_rows.shape[0], tok_ids.shape[1])
        .sum(axis=2)
        .astype(jnp.bfloat16)
    )
    filled = jnp.dot(select, tok_rows, preferred_element_type=jnp.float32).astype(jnp.bfloat16)
    return filled.reshape(expert_count, capacity, tok_rows.shape[1])


def dot16(a, b):
    return jnp.dot(
        a.astype(jnp.bfloat16), b.astype(jnp.bfloat16), preferred_element_type=jnp.float32
    )


def dot32(a, b, dims=(((1,), (0,)), ((), ()))):
    return lax.dot_general(
        a, b, dims, precision=lax.Precision.HIGHEST, preferred_element_type=jnp.float32
    )


def orthonormal_kernel(rows_ref, basis_ref, gram_ref, x_ref):
    rank = rows_ref.shape[1]
    gram = lax.dot_general(
        rows_ref[...], rows_ref[...], (((0,), (0,)), ((), ())), preferred_element_type=jnp.float32
    )
    eye = (
        lax.broadcasted_iota(jnp.int32, (rank, rank), 0)
        == lax.broadcasted_iota(jnp.int32, (rank, rank), 1)
    )
    diagonal = jnp.where(eye, gram, 0.0)
    down = lax.rsqrt(jnp.sum(diagonal, axis=1, keepdims=True))
    across = lax.rsqrt(jnp.sum(diagonal, axis=0, keepdims=True))
    gram = gram * down * across
    gram_ref[...] = gram
    rough = gram.astype(jnp.bfloat16)
    square = dot16(rough, rough)
    inv = lax.rsqrt(1.02 * jnp.sqrt(jnp.sum(square * square)))
    inv2 = inv * inv
    unit = eye.astype(jnp.float32)
    a, b, c = QUINTICS[0]
    x = inv * (a * unit + (b * inv2) * gram + (c * inv2 * inv2) * square)
    for a, b, c in QUINTICS[1:]:
        x16 = x.astype(jnp.bfloat16)
        s16 = dot16(x16, dot16(rough, x16)).astype(jnp.bfloat16)
        x = a * x + dot16(x16, b * s16.astype(jnp.float32) + c * dot16(s16, s16))
    x_ref[...] = x

    def unfinished(state):
        step, size = state
        return (size > DONE) & (step < MOST)

    def refine(state):
        step, _ = state
        x = x_ref[...]
        s = dot32(x, dot32(gram_ref[...], x), (((0,), (0,)), ((), ())))
        e = unit - s
        ee = dot16(e, e)
        x_ref[...] = x + dot16(x, 0.5 * e + 0.375 * ee)
        return step + 1, jnp.sum(ee * ee)

    lax.while_loop(unfinished, refine, (jnp.int32(0), jnp.float32(1.0)))
    scaled = x_ref[...] * down
    high = scaled.astype(jnp.bfloat16)
    low = (scaled - high.astype(jnp.float32)).astype(jnp.bfloat16)
    rows = rows_ref[...]
    basis_ref[...] = (
        jnp.dot(rows, high, preferred_element_type=jnp.float32)
        + jnp.dot(rows, low, preferred_element_type=jnp.float32)
    ).astype(jnp.bfloat16)


def orthonormal(cluster_rows):
    rank = cluster_rows.shape[1]
    return pl.pallas_call(
        orthonormal_kernel,
        out_shape=jax.ShapeDtypeStruct(cluster_rows.shape, jnp.bfloat16),
        in_specs=[pl.BlockSpec(memory_space=pltpu.VMEM)],
        out_specs=pl.BlockSpec(memory_space=pltpu.VMEM),
        scratch_shapes=[
            pltpu.VMEM((rank, rank), jnp.float32),
            pltpu.VMEM((rank, rank), jnp.float32),
        ],
        compiler_params=pltpu.CompilerParams(vmem_limit_bytes=48 << 20),
        cost_estimate=pl.CostEstimate(
            flops=40_000_000_000, bytes_accessed=4 << 20, transcendentals=0
        ),
        name="orthonormal",
    )(cluster_rows)


CHUNKS = 4
TILE = (16, 128)


def exchange_kernel(
    part, same, out, heard, pairs, met, own, tiles, tiles32, mixed32, mixed,
    first_sent, first_got, second_sent, second_got, out_sent, out_got, back_sent, back_got,
    share_sent, share_got,
):
    experts, n_token = lax.axis_size("expert"), lax.axis_size("token")
    me, t = lax.axis_index("expert"), lax.axis_index("token")
    near, far = t + 1 - 2 * (t % 2), n_token - 1 - t
    block = part.shape[0] // n_token
    half = part.shape[1] // 2
    step = block // CHUNKS
    tile_rows, tile_cols = TILE
    halves = (pl.ds(0, half), pl.ds(half, half))

    def place(expert):
        core, chip = expert % 2, expert // 2
        y, z = chip % 4, chip // 4
        return core + 2 * (z % 2), z // 2, y

    def expert_at(chunk, deep, y):
        return ((2 * deep + chunk // 2) * 4 + y) * 2 + chunk % 2

    def tile_at(base, chunk, deep, y):
        row = pl.multiple_of(base + chunk * step + deep * tile_rows, tile_rows)
        return pl.ds(row, tile_rows), pl.ds(pl.multiple_of(y * tile_cols, tile_cols), tile_cols)

    def rows_of(owner, chunk):
        return pl.ds(pl.multiple_of(owner * block + chunk * step, step), step)

    def send(src, dst, sent, got, device):
        return pltpu.make_async_remote_copy(
            src_ref=src, dst_ref=dst, send_sem=sent, recv_sem=got,
            device_id=device, device_id_type=MESH,
        )

    barrier = pltpu.get_barrier_semaphore()

    def greet(i, carry):
        pl.semaphore_signal(
            barrier, inc=1, device_id=((me + i) % experts, t), device_id_type=MESH
        )
        return carry

    for other in (near, far):
        pl.semaphore_signal(barrier, inc=1, device_id=(me, other), device_id_type=MESH)
    lax.fori_loop(1, experts, greet, 0)
    pl.semaphore_wait(barrier, experts + 1)

    def first(chunk, side, slot):
        to = (near, far)[side]
        owner = (to, (n_token - 1 - to, to + 1 - 2 * (to % 2))[side])[slot]
        return send(
            part.at[rows_of(owner, chunk), halves[side]], heard.at[side, chunk, slot],
            first_sent.at[side, chunk, slot], first_got.at[side, chunk, slot], (me, to),
        )

    def second(chunk, side):
        return send(
            pairs.at[side, chunk], met.at[side, chunk],
            second_sent.at[side, chunk], second_got.at[side, chunk], (me, (far, near)[side]),
        )

    def start_first(chunk, carry):
        for side in range(2):
            for slot in (1, 0):
                first(chunk, side, slot).start()
        return carry

    def start_second(chunk):
        for side in range(2):
            first(chunk, side, 1).wait_recv()
            pairs[side, chunk] = (
                part[rows_of((far, near)[side], chunk), halves[side]].astype(jnp.float32)
                + heard[side, chunk, 1].astype(jnp.float32)
            ).astype(jnp.bfloat16)
            second(chunk, side).start()

    def scatter(chunk):
        for side in range(2):
            first(chunk, side, 0).wait_recv()
            second(chunk, side).wait_recv()
            own[pl.ds(pl.multiple_of(chunk * step, step), step), halves[side]] = (
                part[rows_of(t, chunk), halves[side]].astype(jnp.float32)
                + heard[side, chunk, 0].astype(jnp.float32)
                + met[side, chunk].astype(jnp.float32)
            ).astype(jnp.bfloat16)
        count = experts // CHUNKS

        def one(i, carry):
            spot = (i + me) % count
            deep, y = spot // 4, spot % 4
            to = expert_at(chunk, deep, y)
            rows, cols = tile_at(0, chunk, deep, y)

            @pl.when(to != me)
            def _():
                send(own.at[rows, cols], tiles.at[me], out_sent, out_got, (to, t)).start()

            @pl.when(to == me)
            def _():
                pltpu.make_async_copy(own.at[rows, cols], tiles.at[me], out_got).start()

            return carry

        lax.fori_loop(0, count, one, 0)

    lax.fori_loop(0, CHUNKS, start_first, 0)
    start_second(0)

    def along(chunk, carry):
        start_second(chunk)
        scatter(chunk - 1)
        return carry

    lax.fori_loop(1, CHUNKS, along, 0)
    scatter(CHUNKS - 1)

    pltpu.make_async_copy(tiles, tiles, out_got).wait()
    tiles32[...] = tiles[...].reshape(tiles32.shape).astype(jnp.float32)
    for r in range(tile_rows):
        every = pl.ds(r, experts, stride=tile_rows)
        mixed32[every, :] = jnp.dot(
            same[...], tiles32[every, :].astype(jnp.bfloat16), preferred_element_type=jnp.float32
        )
    mixed[...] = mixed32[...].astype(jnp.bfloat16).reshape(mixed.shape)

    my_chunk, my_deep, my_y = place(me)
    my_rows, my_cols = tile_at(t * block, my_chunk, my_deep, my_y)

    def give(i, carry):
        to = (me + i) % experts
        send(
            mixed.at[to], out.at[my_rows, my_cols], back_sent, back_got.at[my_chunk], (to, t)
        ).start()
        return carry

    pltpu.make_async_copy(mixed.at[me], out.at[my_rows, my_cols], back_got.at[my_chunk]).start()
    lax.fori_loop(1, experts, give, 0)

    def share(chunk, kind):
        owner = (t, t, near, far)[kind]
        cols = (pl.ds(0, 2 * half), pl.ds(0, 2 * half), halves[0], halves[1])[kind]
        spot = out.at[rows_of(owner, chunk), cols]
        to = (near, far, far, near)[kind]
        return send(spot, spot, share_sent.at[kind, chunk], share_got.at[kind, chunk], (me, to))

    def start_share(chunk):
        mine = out.at[rows_of(t, chunk), :]
        pltpu.make_async_copy(mine, mine, back_got.at[chunk]).wait()
        share(chunk, 0).start()
        share(chunk, 1).start()

    def pass_on(chunk):
        share(chunk, 0).wait_recv()
        share(chunk, 2).start()
        share(chunk, 1).wait_recv()
        share(chunk, 3).start()

    start_share(0)

    def gather(chunk, carry):
        start_share(chunk)
        pass_on(chunk - 1)
        return carry

    lax.fori_loop(1, CHUNKS, gather, 0)
    pass_on(CHUNKS - 1)

    def finish(chunk, carry):
        for kind in (2, 3):
            share(chunk, kind).wait_recv()
        for kind in range(4):
            share(chunk, kind).wait_send()
        for side in range(2):
            second(chunk, side).wait_send()
            for slot in range(2):
                first(chunk, side, slot).wait_send()
        return carry

    lax.fori_loop(0, CHUNKS, finish, 0)
    most = tiles.at[pl.ds(0, experts - 1)]
    pltpu.make_async_copy(most, most, out_sent).wait()
    pltpu.make_async_copy(most, most, back_sent).wait()


def exchange(partial_term, same):
    rows, rank = partial_term.shape
    experts, n_token = lax.axis_size("expert"), lax.axis_size("token")
    block, half = rows // n_token, rank // 2
    step = block // CHUNKS
    tile_rows, tile_cols = TILE
    vmem = pl.BlockSpec(memory_space=pltpu.VMEM)
    dma = pltpu.SemaphoreType.DMA
    return pl.pallas_call(
        exchange_kernel,
        out_shape=jax.ShapeDtypeStruct((rows, rank), jnp.bfloat16),
        in_specs=[vmem, vmem],
        out_specs=vmem,
        scratch_shapes=[
            pltpu.VMEM((2, CHUNKS, 2, step, half), jnp.bfloat16),
            pltpu.VMEM((2, CHUNKS, step, half), jnp.bfloat16),
            pltpu.VMEM((2, CHUNKS, step, half), jnp.bfloat16),
            pltpu.VMEM((block, rank), jnp.bfloat16),
            pltpu.VMEM((experts, tile_rows, tile_cols), jnp.bfloat16),
            pltpu.VMEM((experts * tile_rows, tile_cols), jnp.float32),
            pltpu.VMEM((experts * tile_rows, tile_cols), jnp.float32),
            pltpu.VMEM((experts, tile_rows, tile_cols), jnp.bfloat16),
            dma((2, CHUNKS, 2)), dma((2, CHUNKS, 2)), dma((2, CHUNKS)), dma((2, CHUNKS)),
            dma, dma, dma, dma((CHUNKS,)), dma((4, CHUNKS)), dma((4, CHUNKS)),
        ],
        compiler_params=pltpu.CompilerParams(
            collective_id=0, has_side_effects=True, vmem_limit_bytes=40 << 20
        ),
        cost_estimate=pl.CostEstimate(
            flops=60_000_000_000, bytes_accessed=8 << 20, transcendentals=0
        ),
        name="exchange",
    )(partial_term, same)


def new_basis(partial_term, same):
    return orthonormal(exchange(partial_term, same))


def per_device(tokens, routes, assign, gate_weight, up_weight, sketch):
    expert_count = lax.axis_size("expert")
    gate_local = gate_weight[0]
    up_local = up_weight[0]
    same = (assign[None, :] == assign[:, None]).astype(jnp.bfloat16)
    partial_term = jnp.dot(up_local, sketch[0], preferred_element_type=jnp.float32).astype(
        jnp.bfloat16
    )
    basis = new_basis(partial_term, same)
    projected = lax.dot_general(
        up_local, basis, (((0,), (0,)), ((), ())), preferred_element_type=jnp.float32
    ).astype(jnp.bfloat16)
    partial_term = jnp.dot(up_local, projected, preferred_element_type=jnp.float32).astype(
        jnp.bfloat16
    )
    basis = new_basis(partial_term, same)
    shard_rows = tokens.shape[0]
    capacity = max(2, 2 * shard_rows * routes.shape[1] // expert_count)
    outgoing = place_tokens(tokens, routes, expert_count, capacity)
    arrived = lax.all_to_all(outgoing, "expert", split_axis=0, concat_axis=0, tiled=True)
    slots_in = lax.all_gather(arrived, "token", axis=0, tiled=True)
    slots_in = slots_in.reshape(-1, tokens.shape[1])
    gate_value = jnp.dot(slots_in, gate_local, preferred_element_type=jnp.float32)
    on_basis = jnp.dot(slots_in, basis, preferred_element_type=jnp.float32).astype(jnp.bfloat16)
    coefficient = lax.dot_general(
        basis, up_local, (((0,), (0,)), ((), ())), preferred_element_type=jnp.float32
    ).astype(jnp.bfloat16)
    merged = jnp.dot(on_basis, coefficient, preferred_element_type=jnp.float32)
    hidden = (jax.nn.silu(gate_value) * merged).astype(jnp.bfloat16)
    return hidden[None]


def solution(mesh):
    return jax.shard_map(
        per_device,
        mesh=mesh,
        in_specs=(
            P(("expert", "token"), None),
            P(("expert", "token"), None),
            P(),
            P("expert", None, "token"),
            P("expert", None, "token"),
            P("expert", "token", None),
        ),
        out_specs=P("expert", None, "token"),
        check_vma=False,
    )
```

```python
import jax
import jax.numpy as jnp
from jax import lax
from jax.experimental import pallas as pl
from jax.experimental.pallas import tpu as pltpu
from jax.sharding import PartitionSpec as P

MESH = pl.DeviceIdType.MESH

QUINTICS = (
    (6.009771924945882, -15.455931527233346, 10.973255328070678),
    (2.240850259026762, -1.6147116422452963, 0.4129695492489308),
    (1.8859120675161938, -1.2620718053405737, 0.3762092163333401),
)
DONE = 0.01**2
MOST = 60
OVER_ROWS = (((0,), (0,)), ((), ()))
SLOT_ROWS = 256


def own_slots(tokens, routes):
    expert_count = lax.axis_size("expert")
    rows, width = tokens.shape
    top = routes.shape[1]
    capacity = max(2, 2 * rows * top // expert_count)
    marked = jnp.pad(routes.astype(jnp.bfloat16), ((0, 0), (0, 128 - top)), constant_values=-1)
    every = lax.all_gather(
        jnp.concatenate([tokens, marked], axis=1), "expert", axis=0, tiled=True
    )
    me = lax.axis_index("expert").astype(jnp.bfloat16)
    named = jnp.any(every[:, width:] == me, axis=1).reshape(expert_count, rows)
    before = jnp.arange(rows)[:, None] < jnp.arange(rows)[None, :]
    slot = jnp.sum((named[:, :, None] & before[None]).astype(jnp.int32), axis=1)
    target = jnp.arange(expert_count, dtype=jnp.int32)[:, None] * capacity + slot
    target = jnp.where(named & (slot < capacity), target, -1).reshape(1, -1)
    place = jnp.arange(expert_count * capacity, dtype=jnp.int32)[:, None]
    select = (place == target).astype(jnp.bfloat16)
    picked = jnp.dot(select, every, preferred_element_type=jnp.float32)
    return picked[:, :width].astype(jnp.bfloat16)


def dot16(a, b):
    return jnp.dot(
        a.astype(jnp.bfloat16), b.astype(jnp.bfloat16), preferred_element_type=jnp.float32
    )


def dot32(a, b, dims=(((1,), (0,)), ((), ()))):
    return lax.dot_general(
        a, b, dims, precision=lax.Precision.HIGHEST, preferred_element_type=jnp.float32
    )


def orthonormal(rows_ref, basis_ref, gram_ref, x_ref):
    rank = rows_ref.shape[1]
    gram = lax.dot_general(
        rows_ref[...], rows_ref[...], (((0,), (0,)), ((), ())), preferred_element_type=jnp.float32
    )
    eye = (
        lax.broadcasted_iota(jnp.int32, (rank, rank), 0)
        == lax.broadcasted_iota(jnp.int32, (rank, rank), 1)
    )
    diagonal = jnp.where(eye, gram, 0.0)
    down = lax.rsqrt(jnp.sum(diagonal, axis=1, keepdims=True))
    across = lax.rsqrt(jnp.sum(diagonal, axis=0, keepdims=True))
    gram = gram * down * across
    gram_ref[...] = gram
    rough = gram.astype(jnp.bfloat16)
    square = dot16(rough, rough)
    inv = lax.rsqrt(1.02 * jnp.sqrt(jnp.sum(square * square)))
    inv2 = inv * inv
    unit = eye.astype(jnp.float32)
    a, b, c = QUINTICS[0]
    x = inv * (a * unit + (b * inv2) * gram + (c * inv2 * inv2) * square)
    for a, b, c in QUINTICS[1:]:
        x16 = x.astype(jnp.bfloat16)
        s16 = dot16(x16, dot16(rough, x16)).astype(jnp.bfloat16)
        x = a * x + dot16(x16, b * s16.astype(jnp.float32) + c * dot16(s16, s16))
    x_ref[...] = x

    def unfinished(state):
        step, size = state
        return (size > DONE) & (step < MOST)

    def refine(state):
        step, _ = state
        x = x_ref[...]
        s = dot32(x, dot32(gram_ref[...], x), (((0,), (0,)), ((), ())))
        e = unit - s
        ee = dot16(e, e)
        x_ref[...] = x + dot16(x, 0.5 * e + 0.375 * ee)
        return step + 1, jnp.sum(ee * ee)

    lax.while_loop(unfinished, refine, (jnp.int32(0), jnp.float32(1.0)))
    scaled = x_ref[...] * down
    high = scaled.astype(jnp.bfloat16)
    low = (scaled - high.astype(jnp.float32)).astype(jnp.bfloat16)
    rows = rows_ref[...]
    basis_ref[...] = (
        jnp.dot(rows, high, preferred_element_type=jnp.float32)
        + jnp.dot(rows, low, preferred_element_type=jnp.float32)
    ).astype(jnp.bfloat16)


def gram_kernel(rows_ref, up_ref, projected_ref, basis_ref, gram_ref, x_ref):
    orthonormal(rows_ref, basis_ref, gram_ref, x_ref)
    projected_ref[...] = lax.dot_general(
        up_ref[...], basis_ref[...], OVER_ROWS, preferred_element_type=jnp.float32
    ).astype(jnp.bfloat16)


def hidden_kernel(
    rows_ref, up_ref, gate_ref, slots_ref, hidden_ref, basis_ref, gram_ref, x_ref, coefficient_ref
):
    orthonormal(rows_ref, basis_ref, gram_ref, x_ref)
    coefficient_ref[...] = lax.dot_general(
        basis_ref[...], up_ref[...], OVER_ROWS, preferred_element_type=jnp.float32
    ).astype(jnp.bfloat16)

    def some(i, carry):
        these = pl.ds(pl.multiple_of(i * SLOT_ROWS, SLOT_ROWS), SLOT_ROWS)
        slots = slots_ref[these, :]
        gate = jnp.dot(slots, gate_ref[...], preferred_element_type=jnp.float32)
        on_basis = jnp.dot(slots, basis_ref[...], preferred_element_type=jnp.float32)
        merged = jnp.dot(
            on_basis.astype(jnp.bfloat16),
            coefficient_ref[...],
            preferred_element_type=jnp.float32,
        )
        hidden_ref[these, :] = (gate / (1.0 + jnp.exp(-gate)) * merged).astype(jnp.bfloat16)
        return carry

    lax.fori_loop(0, slots_ref.shape[0] // SLOT_ROWS, some, 0)


def with_basis(kernel, name, out, rank, more, *operands):
    vmem = pl.BlockSpec(memory_space=pltpu.VMEM)
    return pl.pallas_call(
        kernel,
        out_shape=jax.ShapeDtypeStruct(out, jnp.bfloat16),
        in_specs=[vmem] * len(operands),
        out_specs=vmem,
        scratch_shapes=[
            pltpu.VMEM(operands[0].shape, jnp.bfloat16),
            pltpu.VMEM((rank, rank), jnp.float32),
            pltpu.VMEM((rank, rank), jnp.float32),
            *more,
        ],
        compiler_params=pltpu.CompilerParams(vmem_limit_bytes=30 << 20),
        cost_estimate=pl.CostEstimate(
            flops=20_000_000_000, bytes_accessed=8 << 20, transcendentals=0
        ),
        name=name,
    )(*operands)


CHUNKS = 4
AHEAD = 2
TILE = (16, 128)


def exchange_kernel(
    up, right, same, out, part, heard, pairs, met, own, tiles, tiles32, mixed32, mixed,
    first_sent, first_got, second_sent, second_got, out_sent, out_got, back_sent, back_got,
    share_sent, share_got,
):
    experts, n_token = lax.axis_size("expert"), lax.axis_size("token")
    me, t = lax.axis_index("expert"), lax.axis_index("token")
    near, far = t + 1 - 2 * (t % 2), n_token - 1 - t
    block = part.shape[0] // n_token
    half = part.shape[1] // 2
    step = block // CHUNKS
    tile_rows, tile_cols = TILE
    halves = (pl.ds(0, half), pl.ds(half, half))

    def place(expert):
        core, chip = expert % 2, expert // 2
        y, z = chip % 4, chip // 4
        return core + 2 * (z % 2), z // 2, y

    def expert_at(chunk, deep, y):
        return ((2 * deep + chunk // 2) * 4 + y) * 2 + chunk % 2

    def tile_at(base, chunk, deep, y):
        row = pl.multiple_of(base + chunk * step + deep * tile_rows, tile_rows)
        return pl.ds(row, tile_rows), pl.ds(pl.multiple_of(y * tile_cols, tile_cols), tile_cols)

    def rows_of(owner, chunk):
        return pl.ds(pl.multiple_of(owner * block + chunk * step, step), step)

    def send(src, dst, sent, got, device):
        return pltpu.make_async_remote_copy(
            src_ref=src, dst_ref=dst, send_sem=sent, recv_sem=got,
            device_id=device, device_id_type=MESH,
        )

    barrier = pltpu.get_barrier_semaphore()

    def greet(i, carry):
        pl.semaphore_signal(
            barrier, inc=1, device_id=((me + i) % experts, t), device_id_type=MESH
        )
        return carry

    for other in (near, far):
        pl.semaphore_signal(barrier, inc=1, device_id=(me, other), device_id_type=MESH)
    lax.fori_loop(1, experts, greet, 0)

    def multiply(i, carry):
        rows = pl.ds(pl.multiple_of(i * block, block), block)
        part[rows, :] = jnp.dot(
            up[rows, :], right[...], preferred_element_type=jnp.float32
        ).astype(jnp.bfloat16)
        return carry

    lax.fori_loop(0, n_token, multiply, 0)
    pl.semaphore_wait(barrier, experts + 1)

    def first(chunk, side, slot):
        to = (near, far)[side]
        owner = (to, (n_token - 1 - to, to + 1 - 2 * (to % 2))[side])[slot]
        return send(
            part.at[rows_of(owner, chunk), halves[side]], heard.at[side, chunk, slot],
            first_sent.at[side, chunk, slot], first_got.at[side, chunk, slot], (me, to),
        )

    def second(chunk, side):
        return send(
            pairs.at[side, chunk], met.at[side, chunk],
            second_sent.at[side, chunk], second_got.at[side, chunk], (me, (far, near)[side]),
        )

    def start_first(chunk):
        for side in range(2):
            for slot in (1, 0):
                first(chunk, side, slot).start()

    def start_second(chunk):
        for side in range(2):
            first(chunk, side, 1).wait_recv()
            pairs[side, chunk] = (
                part[rows_of((far, near)[side], chunk), halves[side]].astype(jnp.float32)
                + heard[side, chunk, 1].astype(jnp.float32)
            ).astype(jnp.bfloat16)
            second(chunk, side).start()

    def scatter(chunk):
        for side in range(2):
            first(chunk, side, 0).wait_recv()
            second(chunk, side).wait_recv()
            own[pl.ds(pl.multiple_of(chunk * step, step), step), halves[side]] = (
                part[rows_of(t, chunk), halves[side]].astype(jnp.float32)
                + heard[side, chunk, 0].astype(jnp.float32)
                + met[side, chunk].astype(jnp.float32)
            ).astype(jnp.bfloat16)
        count = experts // CHUNKS

        def one(i, carry):
            spot = (i + me) % count
            deep, y = spot // 4, spot % 4
            to = expert_at(chunk, deep, y)
            rows, cols = tile_at(0, chunk, deep, y)

            @pl.when(to != me)
            def _():
                send(own.at[rows, cols], tiles.at[me], out_sent, out_got, (to, t)).start()

            @pl.when(to == me)
            def _():
                pltpu.make_async_copy(own.at[rows, cols], tiles.at[me], out_got).start()

            return carry

        lax.fori_loop(0, count, one, 0)

    my_chunk, my_deep, my_y = place(me)
    my_rows, my_cols = tile_at(t * block, my_chunk, my_deep, my_y)

    def give(i, carry):
        to = (me + i) % experts
        send(
            mixed.at[to], out.at[my_rows, my_cols], back_sent, back_got.at[my_chunk], (to, t)
        ).start()
        return carry

    def give_back():
        pltpu.make_async_copy(tiles, tiles, out_got).wait()
        tiles32[...] = tiles[...].reshape(tiles32.shape).astype(jnp.float32)
        for r in range(tile_rows):
            every = pl.ds(r, experts, stride=tile_rows)
            mixed32[every, :] = jnp.dot(
                same[...],
                tiles32[every, :].astype(jnp.bfloat16),
                preferred_element_type=jnp.float32,
            )
        mixed[...] = mixed32[...].astype(jnp.bfloat16).reshape(mixed.shape)
        pltpu.make_async_copy(mixed.at[me], out.at[my_rows, my_cols], back_got.at[my_chunk]).start()
        lax.fori_loop(1, experts, give, 0)

    for chunk in range(AHEAD):
        start_first(chunk)

    def along(chunk, carry):
        @pl.when(chunk < CHUNKS)
        def _():
            start_second(chunk)

        @pl.when(chunk + AHEAD < CHUNKS)
        def _():
            start_first(chunk + AHEAD)

        @pl.when(chunk > 0)
        def _():
            scatter(chunk - 1)

        return carry

    lax.fori_loop(0, CHUNKS + 1, along, 0)
    give_back()

    def share(chunk, kind):
        owner = (t, t, near, far)[kind]
        cols = (pl.ds(0, 2 * half), pl.ds(0, 2 * half), halves[0], halves[1])[kind]
        spot = out.at[rows_of(owner, chunk), cols]
        to = (near, far, far, near)[kind]
        return send(spot, spot, share_sent.at[kind, chunk], share_got.at[kind, chunk], (me, to))

    def start_share(chunk):
        mine = out.at[rows_of(t, chunk), :]
        pltpu.make_async_copy(mine, mine, back_got.at[chunk]).wait()
        share(chunk, 0).start()
        share(chunk, 1).start()

    def pass_on(chunk):
        share(chunk, 0).wait_recv()
        share(chunk, 2).start()
        share(chunk, 1).wait_recv()
        share(chunk, 3).start()

    start_share(0)

    def gather(chunk, carry):
        start_share(chunk)
        pass_on(chunk - 1)
        return carry

    lax.fori_loop(1, CHUNKS, gather, 0)
    pass_on(CHUNKS - 1)

    def finish(chunk, carry):
        for kind in (2, 3):
            share(chunk, kind).wait_recv()
        for kind in range(4):
            share(chunk, kind).wait_send()
        for side in range(2):
            second(chunk, side).wait_send()
            for slot in range(2):
                first(chunk, side, slot).wait_send()
        return carry

    lax.fori_loop(0, CHUNKS, finish, 0)
    most = tiles.at[pl.ds(0, experts - 1)]
    pltpu.make_async_copy(most, most, out_sent).wait()
    pltpu.make_async_copy(most, most, back_sent).wait()


def exchange(up, right, same):
    rows, rank = up.shape[0], right.shape[1]
    experts, n_token = lax.axis_size("expert"), lax.axis_size("token")
    block, half = rows // n_token, rank // 2
    step = block // CHUNKS
    tile_rows, tile_cols = TILE
    vmem = pl.BlockSpec(memory_space=pltpu.VMEM)
    dma = pltpu.SemaphoreType.DMA
    return pl.pallas_call(
        exchange_kernel,
        out_shape=jax.ShapeDtypeStruct((rows, rank), jnp.bfloat16),
        in_specs=[vmem, vmem, vmem],
        out_specs=vmem,
        scratch_shapes=[
            pltpu.VMEM((rows, rank), jnp.bfloat16),
            pltpu.VMEM((2, CHUNKS, 2, step, half), jnp.bfloat16),
            pltpu.VMEM((2, CHUNKS, step, half), jnp.bfloat16),
            pltpu.VMEM((2, CHUNKS, step, half), jnp.bfloat16),
            pltpu.VMEM((block, rank), jnp.bfloat16),
            pltpu.VMEM((experts, tile_rows, tile_cols), jnp.bfloat16),
            pltpu.VMEM((experts * tile_rows, tile_cols), jnp.float32),
            pltpu.VMEM((experts * tile_rows, tile_cols), jnp.float32),
            pltpu.VMEM((experts, tile_rows, tile_cols), jnp.bfloat16),
            dma((2, CHUNKS, 2)), dma((2, CHUNKS, 2)), dma((2, CHUNKS)), dma((2, CHUNKS)),
            dma, dma, dma, dma((CHUNKS,)), dma((4, CHUNKS)), dma((4, CHUNKS)),
        ],
        compiler_params=pltpu.CompilerParams(
            collective_id=0, has_side_effects=True, vmem_limit_bytes=20 << 20
        ),
        cost_estimate=pl.CostEstimate(
            flops=60_000_000_000, bytes_accessed=8 << 20, transcendentals=0
        ),
        name="exchange",
    )(up, right, same)


def per_device(tokens, routes, assign, gate_weight, up_weight, sketch):
    gate, up = gate_weight[0], up_weight[0]
    columns, rank = up.shape[1], sketch.shape[2]
    same = (assign[None, :] == assign[:, None]).astype(jnp.bfloat16)
    rows = exchange(up, sketch[0], same)
    projected = with_basis(gram_kernel, "gram", (columns, rank), rank, [], rows, up)
    slots_in = lax.all_gather(own_slots(tokens, routes), "token", axis=0, tiled=True)
    rows = exchange(up, projected, same)
    hidden = with_basis(
        hidden_kernel,
        "hidden",
        (slots_in.shape[0], columns),
        rank,
        [pltpu.VMEM((rank, columns), jnp.bfloat16)],
        rows,
        up,
        gate,
        slots_in,
    )
    return hidden[None]


def solution(mesh):
    return jax.shard_map(
        per_device,
        mesh=mesh,
        in_specs=(
            P(("expert", "token"), None),
            P(("expert", "token"), None),
            P(),
            P("expert", None, "token"),
            P("expert", None, "token"),
            P("expert", "token", None),
        ),
        out_specs=P("expert", None, "token"),
        check_vma=False,
    )
```

```python
import jax
import jax.numpy as jnp
from jax import lax
from jax.experimental import pallas as pl
from jax.experimental.pallas import tpu as pltpu
from jax.sharding import PartitionSpec as P

MESH = pl.DeviceIdType.MESH

QUINTICS = (
    (6.009771924945882, -15.455931527233346, 10.973255328070678),
    (2.240850259026762, -1.6147116422452963, 0.4129695492489308),
    (1.8859120675161938, -1.2620718053405737, 0.3762092163333401),
)
DONE = 0.01**2
MOST = 60
OVER_ROWS = (((0,), (0,)), ((), ()))
SLOT_ROWS = 256
PLANE = 8


def line_tokens(tokens, routes):
    expert_count = lax.axis_size("expert")
    planes = expert_count // PLANE
    top = routes.shape[1]
    marked = jnp.pad(routes.astype(jnp.bfloat16), ((0, 0), (0, 128 - top)), constant_values=-1)
    return lax.all_gather(
        jnp.concatenate([tokens, marked], axis=1),
        "expert",
        axis=0,
        tiled=True,
        axis_index_groups=[[z * PLANE + i for z in range(planes)] for i in range(PLANE)],
    )


def picked_slots(every, rows, width, capacity):
    planes = every.shape[0] // rows
    me = lax.axis_index("expert")
    spot = me % PLANE
    turn = jnp.arange(PLANE, dtype=jnp.int32)
    to = (me - spot + (spot + turn) % PLANE).astype(jnp.bfloat16)
    named = jnp.any(every[None, :, width:] == to[:, None, None], axis=2)
    n = jnp.arange(planes * rows, dtype=jnp.int32)
    before = (n[:, None] < n[None, :]) & (n[:, None] // rows == n[None, :] // rows)
    slot = jnp.dot(
        named.astype(jnp.bfloat16), before.astype(jnp.bfloat16), preferred_element_type=jnp.float32
    ).astype(jnp.int32)
    target = jnp.where(named & (slot < capacity), n[None, :] // rows * capacity + slot, -1)
    place = jnp.arange(planes * capacity, dtype=jnp.int32)
    select = (place[None, :, None] == target[:, None, :]).astype(jnp.bfloat16)
    picked = jnp.dot(
        select.reshape(-1, planes * rows), every[:, :width], preferred_element_type=jnp.float32
    ).astype(jnp.bfloat16)
    return picked.reshape(PLANE, planes * capacity, width)


def plane_slots(picked):
    expert_count = lax.axis_size("expert")
    came = [picked[0]]
    for i in range(1, PLANE):
        pairs = [(e, e - e % PLANE + (e % PLANE + i) % PLANE) for e in range(expert_count)]
        came.append(lax.ppermute(picked[i], "expert", pairs))
    return came


def ordered_slots(came, capacity):
    planes = lax.axis_size("expert") // PLANE
    spot = lax.axis_index("expert") % PLANE
    source = jnp.arange(PLANE * planes * capacity, dtype=jnp.int32)
    sender = (spot + PLANE - source // (planes * capacity)) % PLANE
    z, s = source // capacity % planes, source % capacity
    order = (source[:, None] == ((z * PLANE + sender) * capacity + s)[None, :]).astype(jnp.bfloat16)
    return jnp.dot(
        order, jnp.concatenate(came, axis=0), preferred_element_type=jnp.float32
    ).astype(jnp.bfloat16)


def dot16(a, b):
    return jnp.dot(
        a.astype(jnp.bfloat16), b.astype(jnp.bfloat16), preferred_element_type=jnp.float32
    )


def dot32(a, b, dims=(((1,), (0,)), ((), ()))):
    return lax.dot_general(
        a, b, dims, precision=lax.Precision.HIGHEST, preferred_element_type=jnp.float32
    )


def orthonormal(rows_ref, basis_ref, gram_ref, x_ref):
    rank = rows_ref.shape[1]
    gram = lax.dot_general(
        rows_ref[...], rows_ref[...], (((0,), (0,)), ((), ())), preferred_element_type=jnp.float32
    )
    eye = (
        lax.broadcasted_iota(jnp.int32, (rank, rank), 0)
        == lax.broadcasted_iota(jnp.int32, (rank, rank), 1)
    )
    diagonal = jnp.where(eye, gram, 0.0)
    down = lax.rsqrt(jnp.sum(diagonal, axis=1, keepdims=True))
    across = lax.rsqrt(jnp.sum(diagonal, axis=0, keepdims=True))
    gram = gram * down * across
    gram_ref[...] = gram
    rough = gram.astype(jnp.bfloat16)
    square = dot16(rough, rough)
    inv = lax.rsqrt(1.02 * jnp.sqrt(jnp.sum(square * square)))
    inv2 = inv * inv
    unit = eye.astype(jnp.float32)
    a, b, c = QUINTICS[0]
    x = inv * (a * unit + (b * inv2) * gram + (c * inv2 * inv2) * square)
    for a, b, c in QUINTICS[1:]:
        x16 = x.astype(jnp.bfloat16)
        s16 = dot16(x16, dot16(rough, x16)).astype(jnp.bfloat16)
        x = a * x + dot16(x16, b * s16.astype(jnp.float32) + c * dot16(s16, s16))
    x_ref[...] = x

    def unfinished(state):
        step, size = state
        return (size > DONE) & (step < MOST)

    def refine(state):
        step, _ = state
        x = x_ref[...]
        s = dot32(x, dot32(gram_ref[...], x), (((0,), (0,)), ((), ())))
        e = unit - s
        ee = dot16(e, e)
        x_ref[...] = x + dot16(x, 0.5 * e + 0.375 * ee)
        return step + 1, jnp.sum(ee * ee)

    lax.while_loop(unfinished, refine, (jnp.int32(0), jnp.float32(1.0)))
    scaled = x_ref[...] * down
    high = scaled.astype(jnp.bfloat16)
    low = (scaled - high.astype(jnp.float32)).astype(jnp.bfloat16)
    rows = rows_ref[...]
    basis_ref[...] = (
        jnp.dot(rows, high, preferred_element_type=jnp.float32)
        + jnp.dot(rows, low, preferred_element_type=jnp.float32)
    ).astype(jnp.bfloat16)


def gram_kernel(rows_ref, up_ref, projected_ref, basis_ref, gram_ref, x_ref):
    orthonormal(rows_ref, basis_ref, gram_ref, x_ref)
    projected_ref[...] = lax.dot_general(
        up_ref[...], basis_ref[...], OVER_ROWS, preferred_element_type=jnp.float32
    ).astype(jnp.bfloat16)


def hidden_kernel(
    rows_ref, up_ref, gate_ref, slots_ref, hidden_ref, basis_ref, gram_ref, x_ref, coefficient_ref
):
    orthonormal(rows_ref, basis_ref, gram_ref, x_ref)
    coefficient_ref[...] = lax.dot_general(
        basis_ref[...], up_ref[...], OVER_ROWS, preferred_element_type=jnp.float32
    ).astype(jnp.bfloat16)

    def some(i, carry):
        these = pl.ds(pl.multiple_of(i * SLOT_ROWS, SLOT_ROWS), SLOT_ROWS)
        slots = slots_ref[these, :]
        gate = jnp.dot(slots, gate_ref[...], preferred_element_type=jnp.float32)
        on_basis = jnp.dot(slots, basis_ref[...], preferred_element_type=jnp.float32)
        merged = jnp.dot(
            on_basis.astype(jnp.bfloat16),
            coefficient_ref[...],
            preferred_element_type=jnp.float32,
        )
        hidden_ref[these, :] = (gate / (1.0 + jnp.exp(-gate)) * merged).astype(jnp.bfloat16)
        return carry

    lax.fori_loop(0, slots_ref.shape[0] // SLOT_ROWS, some, 0)


def with_basis(kernel, name, out, rank, more, *operands):
    vmem = pl.BlockSpec(memory_space=pltpu.VMEM)
    return pl.pallas_call(
        kernel,
        out_shape=jax.ShapeDtypeStruct(out, jnp.bfloat16),
        in_specs=[vmem] * len(operands),
        out_specs=vmem,
        scratch_shapes=[
            pltpu.VMEM(operands[0].shape, jnp.bfloat16),
            pltpu.VMEM((rank, rank), jnp.float32),
            pltpu.VMEM((rank, rank), jnp.float32),
            *more,
        ],
        compiler_params=pltpu.CompilerParams(vmem_limit_bytes=30 << 20),
        cost_estimate=pl.CostEstimate(
            flops=20_000_000_000, bytes_accessed=8 << 20, transcendentals=0
        ),
        name=name,
    )(*operands)


CHUNKS = 4
AHEAD = 2
TILE = (16, 128)


def exchange_kernel(
    up, right, same, out, part, heard, pairs, met, own, tiles, tiles32, mixed32, mixed,
    first_sent, first_got, second_sent, second_got, out_sent, out_got, back_sent, back_got,
    share_sent, share_got,
):
    experts, n_token = lax.axis_size("expert"), lax.axis_size("token")
    me, t = lax.axis_index("expert"), lax.axis_index("token")
    near, far = t + 1 - 2 * (t % 2), n_token - 1 - t
    block = part.shape[0] // n_token
    half = part.shape[1] // 2
    step = block // CHUNKS
    tile_rows, tile_cols = TILE
    halves = (pl.ds(0, half), pl.ds(half, half))

    def place(expert):
        core, chip = expert % 2, expert // 2
        y, z = chip % 4, chip // 4
        return core + 2 * (z % 2), z // 2, y

    def expert_at(chunk, deep, y):
        return ((2 * deep + chunk // 2) * 4 + y) * 2 + chunk % 2

    def tile_at(base, chunk, deep, y):
        row = pl.multiple_of(base + chunk * step + deep * tile_rows, tile_rows)
        return pl.ds(row, tile_rows), pl.ds(pl.multiple_of(y * tile_cols, tile_cols), tile_cols)

    def rows_of(owner, chunk):
        return pl.ds(pl.multiple_of(owner * block + chunk * step, step), step)

    def send(src, dst, sent, got, device):
        return pltpu.make_async_remote_copy(
            src_ref=src, dst_ref=dst, send_sem=sent, recv_sem=got,
            device_id=device, device_id_type=MESH,
        )

    barrier = pltpu.get_barrier_semaphore()

    def greet(i, carry):
        pl.semaphore_signal(
            barrier, inc=1, device_id=((me + i) % experts, t), device_id_type=MESH
        )
        return carry

    for other in (near, far):
        pl.semaphore_signal(barrier, inc=1, device_id=(me, other), device_id_type=MESH)
    lax.fori_loop(1, experts, greet, 0)

    def multiply(i, carry):
        rows = pl.ds(pl.multiple_of(i * block, block), block)
        part[rows, :] = jnp.dot(
            up[rows, :], right[...], preferred_element_type=jnp.float32
        ).astype(jnp.bfloat16)
        return carry

    lax.fori_loop(0, n_token, multiply, 0)
    pl.semaphore_wait(barrier, experts + 1)

    def first(chunk, side, slot):
        to = (near, far)[side]
        owner = (to, (n_token - 1 - to, to + 1 - 2 * (to % 2))[side])[slot]
        return send(
            part.at[rows_of(owner, chunk), halves[side]], heard.at[side, chunk, slot],
            first_sent.at[side, chunk, slot], first_got.at[side, chunk, slot], (me, to),
        )

    def second(chunk, side):
        return send(
            pairs.at[side, chunk], met.at[side, chunk],
            second_sent.at[side, chunk], second_got.at[side, chunk], (me, (far, near)[side]),
        )

    def start_first(chunk):
        for side in range(2):
            for slot in (1, 0):
                first(chunk, side, slot).start()

    def start_second(chunk):
        for side in range(2):
            first(chunk, side, 1).wait_recv()
            pairs[side, chunk] = (
                part[rows_of((far, near)[side], chunk), halves[side]].astype(jnp.float32)
                + heard[side, chunk, 1].astype(jnp.float32)
            ).astype(jnp.bfloat16)
            second(chunk, side).start()

    def scatter(chunk):
        for side in range(2):
            first(chunk, side, 0).wait_recv()
            second(chunk, side).wait_recv()
            own[pl.ds(pl.multiple_of(chunk * step, step), step), halves[side]] = (
                part[rows_of(t, chunk), halves[side]].astype(jnp.float32)
                + heard[side, chunk, 0].astype(jnp.float32)
                + met[side, chunk].astype(jnp.float32)
            ).astype(jnp.bfloat16)
        count = experts // CHUNKS

        def one(i, carry):
            spot = (i + me) % count
            deep, y = spot // 4, spot % 4
            to = expert_at(chunk, deep, y)
            rows, cols = tile_at(0, chunk, deep, y)

            @pl.when(to != me)
            def _():
                send(own.at[rows, cols], tiles.at[me], out_sent, out_got, (to, t)).start()

            @pl.when(to == me)
            def _():
                pltpu.make_async_copy(own.at[rows, cols], tiles.at[me], out_got).start()

            return carry

        lax.fori_loop(0, count, one, 0)

    my_chunk, my_deep, my_y = place(me)
    my_rows, my_cols = tile_at(t * block, my_chunk, my_deep, my_y)

    def give(i, carry):
        to = (me + i) % experts
        send(
            mixed.at[to], out.at[my_rows, my_cols], back_sent, back_got.at[my_chunk], (to, t)
        ).start()
        return carry

    def give_back():
        pltpu.make_async_copy(tiles, tiles, out_got).wait()
        tiles32[...] = tiles[...].reshape(tiles32.shape).astype(jnp.float32)
        for r in range(tile_rows):
            every = pl.ds(r, experts, stride=tile_rows)
            mixed32[every, :] = jnp.dot(
                same[...],
                tiles32[every, :].astype(jnp.bfloat16),
                preferred_element_type=jnp.float32,
            )
        mixed[...] = mixed32[...].astype(jnp.bfloat16).reshape(mixed.shape)
        pltpu.make_async_copy(mixed.at[me], out.at[my_rows, my_cols], back_got.at[my_chunk]).start()
        lax.fori_loop(1, experts, give, 0)

    for chunk in range(AHEAD):
        start_first(chunk)

    def along(chunk, carry):
        @pl.when(chunk < CHUNKS)
        def _():
            start_second(chunk)

        @pl.when(chunk + AHEAD < CHUNKS)
        def _():
            start_first(chunk + AHEAD)

        @pl.when(chunk > 0)
        def _():
            scatter(chunk - 1)

        return carry

    lax.fori_loop(0, CHUNKS + 1, along, 0)
    give_back()

    def share(chunk, kind):
        owner = (t, t, near, far)[kind]
        cols = (pl.ds(0, 2 * half), pl.ds(0, 2 * half), halves[0], halves[1])[kind]
        spot = out.at[rows_of(owner, chunk), cols]
        to = (near, far, far, near)[kind]
        return send(spot, spot, share_sent.at[kind, chunk], share_got.at[kind, chunk], (me, to))

    def start_share(chunk):
        mine = out.at[rows_of(t, chunk), :]
        pltpu.make_async_copy(mine, mine, back_got.at[chunk]).wait()
        share(chunk, 0).start()
        share(chunk, 1).start()

    def pass_on(chunk):
        share(chunk, 0).wait_recv()
        share(chunk, 2).start()
        share(chunk, 1).wait_recv()
        share(chunk, 3).start()

    start_share(0)

    def gather(chunk, carry):
        start_share(chunk)
        pass_on(chunk - 1)
        return carry

    lax.fori_loop(1, CHUNKS, gather, 0)
    pass_on(CHUNKS - 1)

    def finish(chunk, carry):
        for kind in (2, 3):
            share(chunk, kind).wait_recv()
        for kind in range(4):
            share(chunk, kind).wait_send()
        for side in range(2):
            second(chunk, side).wait_send()
            for slot in range(2):
                first(chunk, side, slot).wait_send()
        return carry

    lax.fori_loop(0, CHUNKS, finish, 0)
    most = tiles.at[pl.ds(0, experts - 1)]
    pltpu.make_async_copy(most, most, out_sent).wait()
    pltpu.make_async_copy(most, most, back_sent).wait()


def exchange(up, right, same):
    rows, rank = up.shape[0], right.shape[1]
    experts, n_token = lax.axis_size("expert"), lax.axis_size("token")
    block, half = rows // n_token, rank // 2
    step = block // CHUNKS
    tile_rows, tile_cols = TILE
    vmem = pl.BlockSpec(memory_space=pltpu.VMEM)
    dma = pltpu.SemaphoreType.DMA
    return pl.pallas_call(
        exchange_kernel,
        out_shape=jax.ShapeDtypeStruct((rows, rank), jnp.bfloat16),
        in_specs=[vmem, vmem, vmem],
        out_specs=vmem,
        scratch_shapes=[
            pltpu.VMEM((rows, rank), jnp.bfloat16),
            pltpu.VMEM((2, CHUNKS, 2, step, half), jnp.bfloat16),
            pltpu.VMEM((2, CHUNKS, step, half), jnp.bfloat16),
            pltpu.VMEM((2, CHUNKS, step, half), jnp.bfloat16),
            pltpu.VMEM((block, rank), jnp.bfloat16),
            pltpu.VMEM((experts, tile_rows, tile_cols), jnp.bfloat16),
            pltpu.VMEM((experts * tile_rows, tile_cols), jnp.float32),
            pltpu.VMEM((experts * tile_rows, tile_cols), jnp.float32),
            pltpu.VMEM((experts, tile_rows, tile_cols), jnp.bfloat16),
            dma((2, CHUNKS, 2)), dma((2, CHUNKS, 2)), dma((2, CHUNKS)), dma((2, CHUNKS)),
            dma, dma, dma, dma((CHUNKS,)), dma((4, CHUNKS)), dma((4, CHUNKS)),
        ],
        compiler_params=pltpu.CompilerParams(
            collective_id=0, has_side_effects=True, vmem_limit_bytes=20 << 20
        ),
        cost_estimate=pl.CostEstimate(
            flops=60_000_000_000, bytes_accessed=8 << 20, transcendentals=0
        ),
        name="exchange",
    )(up, right, same)


def per_device(tokens, routes, assign, gate_weight, up_weight, sketch):
    gate, up = gate_weight[0], up_weight[0]
    columns, rank = up.shape[1], sketch.shape[2]
    same = (assign[None, :] == assign[:, None]).astype(jnp.bfloat16)
    capacity = max(2, 2 * tokens.shape[0] * routes.shape[1] // lax.axis_size("expert"))
    every = line_tokens(tokens, routes)
    rows = exchange(up, sketch[0], same)
    every, rows = lax.optimization_barrier((every, rows))
    picked = picked_slots(every, *tokens.shape, capacity)
    picked, rows = lax.optimization_barrier((picked, rows))
    came = plane_slots(picked)
    projected = with_basis(gram_kernel, "gram", (columns, rank), rank, [], rows, up)
    came, projected = lax.optimization_barrier((came, projected))
    slots, projected = lax.optimization_barrier((ordered_slots(came, capacity), projected))
    slots_in = lax.all_gather(slots, "token", axis=0, tiled=True)
    rows = exchange(up, projected, same)
    hidden = with_basis(
        hidden_kernel,
        "hidden",
        (slots_in.shape[0], columns),
        rank,
        [pltpu.VMEM((rank, columns), jnp.bfloat16)],
        rows,
        up,
        gate,
        slots_in,
    )
    return hidden[None]


def solution(mesh):
    return jax.shard_map(
        per_device,
        mesh=mesh,
        in_specs=(
            P(("expert", "token"), None),
            P(("expert", "token"), None),
            P(),
            P("expert", None, "token"),
            P("expert", None, "token"),
            P("expert", "token", None),
        ),
        out_specs=P("expert", None, "token"),
        check_vma=False,
    )
```

```python
import jax
import jax.numpy as jnp
from jax import lax
from jax.experimental import pallas as pl
from jax.experimental.pallas import tpu as pltpu
from jax.sharding import PartitionSpec as P

MESH = pl.DeviceIdType.MESH

QUINTICS = (
    (6.009771924945882, -15.455931527233346, 10.973255328070678),
    (2.240850259026762, -1.6147116422452963, 0.4129695492489308),
    (1.8859120675161938, -1.2620718053405737, 0.3762092163333401),
)
DONE = 0.01**2
MOST = 60
OVER_ROWS = (((0,), (0,)), ((), ()))
SLOT_ROWS = 256
CORES = 2
LINE = 4
PLANE = LINE * CORES


def line_tokens(tokens, routes):
    expert_count = lax.axis_size("expert")
    planes = expert_count // PLANE
    top = routes.shape[1]
    marked = jnp.pad(routes.astype(jnp.bfloat16), ((0, 0), (0, 128 - top)), constant_values=-1)
    return lax.all_gather(
        jnp.concatenate([tokens, marked], axis=1),
        "expert",
        axis=0,
        tiled=True,
        axis_index_groups=[[z * PLANE + i for z in range(planes)] for i in range(PLANE)],
    )


def picked_slots(every, rows, width, capacity):
    planes = every.shape[0] // rows
    me = lax.axis_index("expert")
    spot = me % PLANE
    turn = jnp.arange(PLANE, dtype=jnp.int32)
    to = me - spot + (spot + turn % LINE * CORES) % PLANE
    to = (to + turn // LINE * (1 - 2 * (me % CORES))).astype(jnp.bfloat16)
    named = jnp.any(every[None, :, width:] == to[:, None, None], axis=2)
    n = jnp.arange(planes * rows, dtype=jnp.int32)
    before = (n[:, None] < n[None, :]) & (n[:, None] // rows == n[None, :] // rows)
    slot = jnp.dot(
        named.astype(jnp.bfloat16), before.astype(jnp.bfloat16), preferred_element_type=jnp.float32
    ).astype(jnp.int32)
    target = jnp.where(named & (slot < capacity), n[None, :] // rows * capacity + slot, -1)
    place = jnp.arange(planes * capacity, dtype=jnp.int32)
    select = (place[None, :, None] == target[:, None, :]).astype(jnp.bfloat16)
    picked = jnp.dot(
        select.reshape(-1, planes * rows), every[:, :width], preferred_element_type=jnp.float32
    ).astype(jnp.bfloat16)
    return picked.reshape(CORES, LINE, planes * capacity, width)


def plane_slots(picked):
    everyone = range(lax.axis_size("expert"))
    mates = [(e, e + 1 - 2 * (e % CORES)) for e in everyone]
    both = jnp.stack([picked[0], lax.ppermute(picked[1], "expert", mates)], axis=1)
    came = [both[0]]
    for i in range(1, LINE):
        pairs = [(e, e - e % PLANE + (e % PLANE + i * CORES) % PLANE) for e in everyone]
        came.append(lax.ppermute(both[i], "expert", pairs))
    return came


def ordered_slots(came, capacity):
    planes = lax.axis_size("expert") // PLANE
    spot = lax.axis_index("expert") % PLANE
    source = jnp.arange(PLANE * planes * capacity, dtype=jnp.int32)
    step = source // (planes * capacity)
    sender = (spot + PLANE - step // CORES * CORES) % PLANE
    sender = sender + step % CORES * (1 - 2 * (spot % CORES))
    z, s = source // capacity % planes, source % capacity
    order = (source[:, None] == ((z * PLANE + sender) * capacity + s)[None, :]).astype(jnp.bfloat16)
    return jnp.dot(
        order, jnp.concatenate(came, axis=0).reshape(source.shape[0], -1), preferred_element_type=jnp.float32
    ).astype(jnp.bfloat16)


def dot16(a, b):
    return jnp.dot(
        a.astype(jnp.bfloat16), b.astype(jnp.bfloat16), preferred_element_type=jnp.float32
    )


def dot32(a, b, dims=(((1,), (0,)), ((), ()))):
    return lax.dot_general(
        a, b, dims, precision=lax.Precision.HIGHEST, preferred_element_type=jnp.float32
    )


def orthonormal(rows_ref, basis_ref, gram_ref, x_ref):
    rank = rows_ref.shape[1]
    gram = lax.dot_general(
        rows_ref[...], rows_ref[...], (((0,), (0,)), ((), ())), preferred_element_type=jnp.float32
    )
    eye = (
        lax.broadcasted_iota(jnp.int32, (rank, rank), 0)
        == lax.broadcasted_iota(jnp.int32, (rank, rank), 1)
    )
    diagonal = jnp.where(eye, gram, 0.0)
    down = lax.rsqrt(jnp.sum(diagonal, axis=1, keepdims=True))
    across = lax.rsqrt(jnp.sum(diagonal, axis=0, keepdims=True))
    gram = gram * down * across
    gram_ref[...] = gram
    rough = gram.astype(jnp.bfloat16)
    square = dot16(rough, rough)
    inv = lax.rsqrt(1.02 * jnp.sqrt(jnp.sum(square * square)))
    inv2 = inv * inv
    unit = eye.astype(jnp.float32)
    a, b, c = QUINTICS[0]
    x = inv * (a * unit + (b * inv2) * gram + (c * inv2 * inv2) * square)
    for a, b, c in QUINTICS[1:]:
        x16 = x.astype(jnp.bfloat16)
        s16 = dot16(x16, dot16(rough, x16)).astype(jnp.bfloat16)
        x = a * x + dot16(x16, b * s16.astype(jnp.float32) + c * dot16(s16, s16))
    x_ref[...] = x

    def unfinished(state):
        step, size = state
        return (size > DONE) & (step < MOST)

    def refine(state):
        step, _ = state
        x = x_ref[...]
        s = dot32(x, dot32(gram_ref[...], x), (((0,), (0,)), ((), ())))
        e = unit - s
        ee = dot16(e, e)
        x_ref[...] = x + dot16(x, 0.5 * e + 0.375 * ee)
        return step + 1, jnp.sum(ee * ee)

    lax.while_loop(unfinished, refine, (jnp.int32(0), jnp.float32(1.0)))
    scaled = x_ref[...] * down
    high = scaled.astype(jnp.bfloat16)
    low = (scaled - high.astype(jnp.float32)).astype(jnp.bfloat16)
    rows = rows_ref[...]
    basis_ref[...] = (
        jnp.dot(rows, high, preferred_element_type=jnp.float32)
        + jnp.dot(rows, low, preferred_element_type=jnp.float32)
    ).astype(jnp.bfloat16)


def gram_kernel(rows_ref, up_ref, projected_ref, basis_ref, gram_ref, x_ref):
    orthonormal(rows_ref, basis_ref, gram_ref, x_ref)
    projected_ref[...] = lax.dot_general(
        up_ref[...], basis_ref[...], OVER_ROWS, preferred_element_type=jnp.float32
    ).astype(jnp.bfloat16)


def hidden_kernel(
    rows_ref, up_ref, gate_ref, slots_hbm, hidden_ref, basis_ref, gram_ref, x_ref, coefficient_ref,
    slots_ref, loaded,
):
    load = pltpu.make_async_copy(slots_hbm, slots_ref, loaded)
    load.start()
    orthonormal(rows_ref, basis_ref, gram_ref, x_ref)
    coefficient_ref[...] = lax.dot_general(
        basis_ref[...], up_ref[...], OVER_ROWS, preferred_element_type=jnp.float32
    ).astype(jnp.bfloat16)

    load.wait()

    def some(i, carry):
        these = pl.ds(pl.multiple_of(i * SLOT_ROWS, SLOT_ROWS), SLOT_ROWS)
        slots = slots_ref[these, :]
        gate = jnp.dot(slots, gate_ref[...], preferred_element_type=jnp.float32)
        on_basis = jnp.dot(slots, basis_ref[...], preferred_element_type=jnp.float32)
        merged = jnp.dot(
            on_basis.astype(jnp.bfloat16),
            coefficient_ref[...],
            preferred_element_type=jnp.float32,
        )
        hidden_ref[these, :] = (gate / (1.0 + jnp.exp(-gate)) * merged).astype(jnp.bfloat16)
        return carry

    lax.fori_loop(0, slots_ref.shape[0] // SLOT_ROWS, some, 0)


def with_basis(kernel, name, out, rank, more, far, *operands):
    vmem = pl.BlockSpec(memory_space=pltpu.VMEM)
    return pl.pallas_call(
        kernel,
        out_shape=jax.ShapeDtypeStruct(out, jnp.bfloat16),
        in_specs=[vmem] * (len(operands) - far) + [pl.BlockSpec(memory_space=pl.ANY)] * far,
        out_specs=vmem,
        scratch_shapes=[
            pltpu.VMEM(operands[0].shape, jnp.bfloat16),
            pltpu.VMEM((rank, rank), jnp.float32),
            pltpu.VMEM((rank, rank), jnp.float32),
            *more,
        ],
        compiler_params=pltpu.CompilerParams(vmem_limit_bytes=(56 if far else 30) << 20),
        cost_estimate=pl.CostEstimate(
            flops=20_000_000_000, bytes_accessed=8 << 20, transcendentals=0
        ),
        name=name,
    )(*operands)


CHUNKS = 4
AHEAD = 2
TILE = (16, 128)


def exchange_kernel(
    up, right, same, out, part, heard, pairs, met, own, tiles, tiles32, mixed32, mixed,
    first_sent, first_got, second_sent, second_got, out_sent, out_got, back_sent, back_got,
    share_sent, share_got,
):
    experts, n_token = lax.axis_size("expert"), lax.axis_size("token")
    me, t = lax.axis_index("expert"), lax.axis_index("token")
    near, far = t + 1 - 2 * (t % 2), n_token - 1 - t
    block = part.shape[0] // n_token
    half = part.shape[1] // 2
    step = block // CHUNKS
    tile_rows, tile_cols = TILE
    halves = (pl.ds(0, half), pl.ds(half, half))

    def place(expert):
        core, chip = expert % 2, expert // 2
        y, z = chip % 4, chip // 4
        return core + 2 * (z % 2), z // 2, y

    def expert_at(chunk, deep, y):
        return ((2 * deep + chunk // 2) * 4 + y) * 2 + chunk % 2

    def tile_at(base, chunk, deep, y):
        row = pl.multiple_of(base + chunk * step + deep * tile_rows, tile_rows)
        return pl.ds(row, tile_rows), pl.ds(pl.multiple_of(y * tile_cols, tile_cols), tile_cols)

    def rows_of(owner, chunk):
        return pl.ds(pl.multiple_of(owner * block + chunk * step, step), step)

    def send(src, dst, sent, got, device):
        return pltpu.make_async_remote_copy(
            src_ref=src, dst_ref=dst, send_sem=sent, recv_sem=got,
            device_id=device, device_id_type=MESH,
        )

    barrier = pltpu.get_barrier_semaphore()

    def greet(i, carry):
        pl.semaphore_signal(
            barrier, inc=1, device_id=((me + i) % experts, t), device_id_type=MESH
        )
        return carry

    for other in (near, far):
        pl.semaphore_signal(barrier, inc=1, device_id=(me, other), device_id_type=MESH)
    lax.fori_loop(1, experts, greet, 0)

    def multiply(i, carry):
        rows = pl.ds(pl.multiple_of(i * block, block), block)
        part[rows, :] = jnp.dot(
            up[rows, :], right[...], preferred_element_type=jnp.float32
        ).astype(jnp.bfloat16)
        return carry

    lax.fori_loop(0, n_token, multiply, 0)
    pl.semaphore_wait(barrier, experts + 1)

    def first(chunk, side, slot):
        to = (near, far)[side]
        owner = (to, (n_token - 1 - to, to + 1 - 2 * (to % 2))[side])[slot]
        return send(
            part.at[rows_of(owner, chunk), halves[side]], heard.at[side, chunk, slot],
            first_sent.at[side, chunk, slot], first_got.at[side, chunk, slot], (me, to),
        )

    def second(chunk, side):
        return send(
            pairs.at[side, chunk], met.at[side, chunk],
            second_sent.at[side, chunk], second_got.at[side, chunk], (me, (far, near)[side]),
        )

    def start_first(chunk):
        for side in range(2):
            for slot in (1, 0):
                first(chunk, side, slot).start()

    def start_second(chunk):
        for side in range(2):
            first(chunk, side, 1).wait_recv()
            pairs[side, chunk] = (
                part[rows_of((far, near)[side], chunk), halves[side]].astype(jnp.float32)
                + heard[side, chunk, 1].astype(jnp.float32)
            ).astype(jnp.bfloat16)
            second(chunk, side).start()

    def scatter(chunk):
        for side in range(2):
            first(chunk, side, 0).wait_recv()
            second(chunk, side).wait_recv()
            own[pl.ds(pl.multiple_of(chunk * step, step), step), halves[side]] = (
                part[rows_of(t, chunk), halves[side]].astype(jnp.float32)
                + heard[side, chunk, 0].astype(jnp.float32)
                + met[side, chunk].astype(jnp.float32)
            ).astype(jnp.bfloat16)
        count = experts // CHUNKS

        def one(i, carry):
            spot = (i + me) % count
            deep, y = spot // 4, spot % 4
            to = expert_at(chunk, deep, y)
            rows, cols = tile_at(0, chunk, deep, y)

            @pl.when(to != me)
            def _():
                send(own.at[rows, cols], tiles.at[me], out_sent, out_got, (to, t)).start()

            @pl.when(to == me)
            def _():
                pltpu.make_async_copy(own.at[rows, cols], tiles.at[me], out_got).start()

            return carry

        lax.fori_loop(0, count, one, 0)

    my_chunk, my_deep, my_y = place(me)
    my_rows, my_cols = tile_at(t * block, my_chunk, my_deep, my_y)

    def give(i, carry):
        to = (me + i) % experts
        send(
            mixed.at[to], out.at[my_rows, my_cols], back_sent, back_got.at[my_chunk], (to, t)
        ).start()
        return carry

    def give_back():
        pltpu.make_async_copy(tiles, tiles, out_got).wait()
        tiles32[...] = tiles[...].reshape(tiles32.shape).astype(jnp.float32)
        for r in range(tile_rows):
            every = pl.ds(r, experts, stride=tile_rows)
            mixed32[every, :] = jnp.dot(
                same[...],
                tiles32[every, :].astype(jnp.bfloat16),
                preferred_element_type=jnp.float32,
            )
        mixed[...] = mixed32[...].astype(jnp.bfloat16).reshape(mixed.shape)
        pltpu.make_async_copy(mixed.at[me], out.at[my_rows, my_cols], back_got.at[my_chunk]).start()
        lax.fori_loop(1, experts, give, 0)

    for chunk in range(AHEAD):
        start_first(chunk)

    def along(chunk, carry):
        @pl.when(chunk < CHUNKS)
        def _():
            start_second(chunk)

        @pl.when(chunk + AHEAD < CHUNKS)
        def _():
            start_first(chunk + AHEAD)

        @pl.when(chunk > 0)
        def _():
            scatter(chunk - 1)

        return carry

    lax.fori_loop(0, CHUNKS + 1, along, 0)
    give_back()

    def share(chunk, kind):
        owner = (t, t, near, far)[kind]
        cols = (pl.ds(0, 2 * half), pl.ds(0, 2 * half), halves[0], halves[1])[kind]
        spot = out.at[rows_of(owner, chunk), cols]
        to = (near, far, far, near)[kind]
        return send(spot, spot, share_sent.at[kind, chunk], share_got.at[kind, chunk], (me, to))

    def start_share(chunk):
        mine = out.at[rows_of(t, chunk), :]
        pltpu.make_async_copy(mine, mine, back_got.at[chunk]).wait()
        share(chunk, 0).start()
        share(chunk, 1).start()

    def pass_on(chunk):
        share(chunk, 0).wait_recv()
        share(chunk, 2).start()
        share(chunk, 1).wait_recv()
        share(chunk, 3).start()

    start_share(0)

    def gather(chunk, carry):
        start_share(chunk)
        pass_on(chunk - 1)
        return carry

    lax.fori_loop(1, CHUNKS, gather, 0)
    pass_on(CHUNKS - 1)

    def finish(chunk, carry):
        for kind in (2, 3):
            share(chunk, kind).wait_recv()
        for kind in range(4):
            share(chunk, kind).wait_send()
        for side in range(2):
            second(chunk, side).wait_send()
            for slot in range(2):
                first(chunk, side, slot).wait_send()
        return carry

    lax.fori_loop(0, CHUNKS, finish, 0)
    most = tiles.at[pl.ds(0, experts - 1)]
    pltpu.make_async_copy(most, most, out_sent).wait()
    pltpu.make_async_copy(most, most, back_sent).wait()


def exchange(up, right, same):
    rows, rank = up.shape[0], right.shape[1]
    experts, n_token = lax.axis_size("expert"), lax.axis_size("token")
    block, half = rows // n_token, rank // 2
    step = block // CHUNKS
    tile_rows, tile_cols = TILE
    vmem = pl.BlockSpec(memory_space=pltpu.VMEM)
    dma = pltpu.SemaphoreType.DMA
    return pl.pallas_call(
        exchange_kernel,
        out_shape=jax.ShapeDtypeStruct((rows, rank), jnp.bfloat16),
        in_specs=[vmem, vmem, vmem],
        out_specs=vmem,
        scratch_shapes=[
            pltpu.VMEM((rows, rank), jnp.bfloat16),
            pltpu.VMEM((2, CHUNKS, 2, step, half), jnp.bfloat16),
            pltpu.VMEM((2, CHUNKS, step, half), jnp.bfloat16),
            pltpu.VMEM((2, CHUNKS, step, half), jnp.bfloat16),
            pltpu.VMEM((block, rank), jnp.bfloat16),
            pltpu.VMEM((experts, tile_rows, tile_cols), jnp.bfloat16),
            pltpu.VMEM((experts * tile_rows, tile_cols), jnp.float32),
            pltpu.VMEM((experts * tile_rows, tile_cols), jnp.float32),
            pltpu.VMEM((experts, tile_rows, tile_cols), jnp.bfloat16),
            dma((2, CHUNKS, 2)), dma((2, CHUNKS, 2)), dma((2, CHUNKS)), dma((2, CHUNKS)),
            dma, dma, dma, dma((CHUNKS,)), dma((4, CHUNKS)), dma((4, CHUNKS)),
        ],
        compiler_params=pltpu.CompilerParams(
            collective_id=0, has_side_effects=True, vmem_limit_bytes=20 << 20
        ),
        cost_estimate=pl.CostEstimate(
            flops=60_000_000_000, bytes_accessed=8 << 20, transcendentals=0
        ),
        name="exchange",
    )(up, right, same)


def per_device(tokens, routes, assign, gate_weight, up_weight, sketch):
    gate, up = gate_weight[0], up_weight[0]
    columns, rank = up.shape[1], sketch.shape[2]
    same = (assign[None, :] == assign[:, None]).astype(jnp.bfloat16)
    capacity = max(2, 2 * tokens.shape[0] * routes.shape[1] // lax.axis_size("expert"))
    every = line_tokens(tokens, routes)
    rows = exchange(up, sketch[0], same)
    every, rows = lax.optimization_barrier((every, rows))
    picked = picked_slots(every, *tokens.shape, capacity)
    picked, rows = lax.optimization_barrier((picked, rows))
    came = plane_slots(picked)
    projected = with_basis(gram_kernel, "gram", (columns, rank), rank, [], 0, rows, up)
    came, projected = lax.optimization_barrier((came, projected))
    slots, projected = lax.optimization_barrier((ordered_slots(came, capacity), projected))
    slots_in = lax.all_gather(slots, "token", axis=0, tiled=True)
    rows = exchange(up, projected, same)
    hidden = with_basis(
        hidden_kernel,
        "hidden",
        (slots_in.shape[0], columns),
        rank,
        [
            pltpu.VMEM((rank, columns), jnp.bfloat16),
            pltpu.VMEM(slots_in.shape, jnp.bfloat16),
            pltpu.SemaphoreType.DMA,
        ],
        1,
        rows,
        up,
        gate,
        slots_in,
    )
    return hidden[None]


def solution(mesh):
    return jax.shard_map(
        per_device,
        mesh=mesh,
        in_specs=(
            P(("expert", "token"), None),
            P(("expert", "token"), None),
            P(),
            P("expert", None, "token"),
            P("expert", None, "token"),
            P("expert", "token", None),
        ),
        out_specs=P("expert", None, "token"),
        check_vma=False,
    )
```
